32 devices in a mesh: section: 8 (over y, x, core), blk: 4 (over z).
Axes of the slice: x: 2, y: 2, z: 4, core: 2. Of those that a mesh axis runs over, the one named last changes fastest.
Arguments:
- images: bfloat16 [64, 65536], P('section', 'blk'), may hold values from 0 to 1
- tile_weights: bfloat16 [8, 512, 4, 128, 128], P('section', 'blk'), may hold values from -0.5 to 0.5
- tile_columns: int32 [8, 512, 4], P('section', 'blk'), may hold values from 0 to 511, as said below
- tile_counts: int32 [8, 512], P('section', 'blk'), may hold values from 1 to 4
- bias: float32 [8, 65536], P('section', 'blk'), may hold values from -0.3 to 0.3
Outputs:
- features: bfloat16 [64, 65536], P('section', 'blk')
The draws below stay inside these ranges and needn't reach their ends.
Inputs may be any that keep to these rules, and one draw needn't show every extreme that they name: `tile_columns`: the column block of every tile differs cyclically (modulo 512) from its row block by at most 64 blocks, and a distance of exactly 64 occurs in every layer on both sides.
All inputs are finite; a program needn't handle non-finite values.
Results may differ from the reference program's by a relative error of at most 0.013.
Values may be sent and summed in bfloat16 or wider, within the bound.
A program may use at most 64 MiB of HBM per device.

```python
import jax
import jax.numpy as jnp

N = 65536
TILE = 128
TILES_ROW = 4
IMAGES = 64
LAYERS = 8
NBLK = 512
SPAN = 64


def draw_tile_columns(key, part):
    key = jax.random.fold_in(key, 11)
    first_key, second_key, third_key = jax.random.split(key, 3)
    offsets = jax.random.randint(first_key, (LAYERS, NBLK, TILES_ROW), -SPAN, SPAN + 1)
    low_rows = jax.random.randint(second_key, (LAYERS,), 0, NBLK)
    high_rows = jax.random.randint(third_key, (LAYERS,), 0, NBLK)
    layer_ids = jnp.arange(LAYERS)
    offsets = offsets.at[layer_ids, low_rows, 0].set(-SPAN)
    offsets = offsets.at[layer_ids, high_rows, 1].set(SPAN)
    row_ids = jnp.arange(NBLK)[None, :, None]
    return ((row_ids + offsets) % NBLK).astype(jnp.int32)


def plant(result, key, smallest, largest):
    shape = result.shape
    spot = [jax.random.randint(jax.random.fold_in(key, axis), (), 0, shape[axis]) for axis in range(len(shape))]
    result = result.at[tuple(spot)].set(smallest)
    longest = shape.index(max(shape))
    spot[longest] = (spot[longest] + 1) % shape[longest]
    return result.at[tuple(spot)].set(largest)


def steps_of(stream_key, dims, cuts, low, high):
    factor_of = 1.0
    for axis_at, parts in cuts:
        heights = jax.random.uniform(jax.random.fold_in(jax.random.fold_in(stream_key, 6), axis_at), (parts,), jnp.float32, low / len(cuts), high / len(cuts))
        factor_of = factor_of * jnp.repeat(jnp.exp(heights), dims[axis_at] // parts).reshape((-1,) + (1,) * (len(dims) - 1 - axis_at))
    return factor_of


def gaussian(stream_key, shape, spread, reach, cuts=(), kind=jnp.bfloat16):
    factor_of = steps_of(stream_key, shape, cuts, -0.22, 0.18) if cuts else 1.0
    result = jax.random.normal(stream_key, shape, jnp.float32) * spread * factor_of
    return jnp.minimum(jnp.maximum(result, -reach), reach).astype(kind)


def setup_inputs(seed: int = 0) -> dict:
    arg_keys = jax.random.split(jax.random.key(seed), 6)
    return {
        "images": jnp.clip(1.0 * jax.random.uniform(arg_keys[0], (IMAGES, N), jnp.float32) ** steps_of(arg_keys[0], (IMAGES, N), ((0, 8), (1, 4)), -0.2, 0.2), 0.0, 1.0).astype(jnp.bfloat16),
        "tile_weights": gaussian(arg_keys[1], (LAYERS, NBLK, TILES_ROW, TILE, TILE), TILE ** -0.5, 0.5, ((0, 8), (1, 4))),
        "tile_columns": draw_tile_columns(jax.random.fold_in(arg_keys[5], 71), 0),
        "tile_counts": plant(jax.random.randint(arg_keys[3], (LAYERS, NBLK), 1, 5), jax.random.fold_in(arg_keys[3], 1), 1, 4).astype(jnp.int32),
        "bias": jnp.clip(jax.random.uniform(arg_keys[4], (LAYERS, N), jnp.float32, -0.3, 0.3) * steps_of(arg_keys[4], (LAYERS, N), ((0, 8), (1, 4)), -0.4, 0.0), -0.3, 0.3),
    }


def reference(images, tile_weights, tile_columns, tile_counts, bias):
    activation = images
    for layer in range(LAYERS):
        column_blocks = activation.reshape(IMAGES, NBLK, TILE).astype(jnp.float32)
        totals = jnp.zeros((IMAGES, NBLK, TILE), jnp.float32)
        for slot in range(TILES_ROW):
            selected = column_blocks[:, tile_columns[layer, :, slot], :]
            live_slot = (tile_counts[layer] > slot).astype(jnp.float32)
            selected = selected * live_slot[None, :, None]
            weight_slice = tile_weights[layer, :, slot].astype(jnp.float32)
            totals = totals + jnp.einsum("irb,rba->ira", selected, weight_slice)
        summed = totals.reshape(IMAGES, N) + bias[layer][None, :]
        activation = jnp.clip(summed, 0.0, 32.0).astype(jnp.bfloat16)
    return activation
```

```python
import functools

import jax
import jax.numpy as jnp
from jax import lax
from jax.experimental import pallas as pl
from jax.experimental.pallas import tpu as pltpu
from jax.sharding import PartitionSpec as P

MESH = pl.DeviceIdType.MESH


def kernel(S, B, R, K, T, UNROLL, idx_ref, bias_ref, images_ref, w_hbm, out_ref, w, homes, landed, snd, *rest):
    exts, (w_sem, home_sem, send_sem, recv_sem, out_sem) = rest[:S], rest[S:]
    s = lax.axis_index("section")
    b = lax.axis_index("blk")
    right, left = lax.rem(b + 1, B), lax.rem(b + B - 1, B)
    H = R // 2
    parts = w_sem.shape[0]
    rows_part = R // parts

    def load(p):
        rows = pl.ds(p * rows_part, rows_part)
        return pltpu.make_async_copy(w_hbm.at[0, rows], w.at[rows], w_sem.at[p])

    for p in range(parts):
        load(p).start()

    barrier = pltpu.get_barrier_semaphore()

    def greet(d, carry):
        to = lax.rem(s + d, S)
        for place in (left, right):
            pl.semaphore_signal(barrier, inc=1, device_id=(to, place), device_id_type=MESH)

        @pl.when(d > 0)
        def _():
            pl.semaphore_signal(barrier, inc=1, device_id=(to, b), device_id_type=MESH)

        return carry

    lax.fori_loop(0, S, greet, 0)

    for ext in exts:
        ext[4 * H] = jnp.zeros(ext.shape[1:], ext.dtype)

    def packed(r, carry):
        homes[r] = images_ref[:, pl.ds(pl.multiple_of(r * T, T), T)]
        return carry

    lax.fori_loop(0, R, packed, 0, unroll=UNROLL)

    pl.semaphore_wait(barrier, 3 * S - 1)

    low, high = pl.ds(0, H), pl.ds(H, H)

    def hops(src, g, to, sem, which):
        half = low if which == 0 else high
        own = exts[g].at[pl.ds(H, H)] if which == 0 else exts[g].at[pl.ds(2 * H, H)]
        halo = exts[g].at[pl.ds(3 * H, H)] if which == 0 else exts[g].at[pl.ds(0, H)]
        place = left if which == 0 else right
        mine = pltpu.make_async_remote_copy(
            src_ref=src.at[half], dst_ref=own, send_sem=sem.at[2 * which], recv_sem=recv_sem.at[g, 2 * which],
            device_id=(to, b), device_id_type=MESH)
        beside = pltpu.make_async_remote_copy(
            src_ref=src.at[half], dst_ref=halo, send_sem=sem.at[2 * which + 1],
            recv_sem=recv_sem.at[g, 2 * which + 1], device_id=(to, place), device_id_type=MESH)
        return mine, beside

    def local(g, which):
        half = low if which == 0 else high
        return pltpu.make_async_copy(
            homes.at[half], exts[g].at[pl.ds((1 + which) * H, H)], recv_sem.at[g, 2 * which])

    for g in range(S):
        @pl.when(s == g)
        def _(g=g):
            for which in (0, 1):
                mine, beside = hops(homes, g, 0, home_sem, which)
                if g == 0:
                    local(g, which).start()
                else:
                    mine.start()
                beside.start()

    def deliver(g, which):
        half = low if which == 0 else high
        return pltpu.make_async_remote_copy(
            src_ref=snd.at[g, half], dst_ref=landed.at[half], send_sem=send_sem.at[g, 2 * which],
            recv_sem=out_sem.at[which], device_id=(g, b), device_id_type=MESH)

    def keep(g, which):
        half = low if which == 0 else high
        return pltpu.make_async_copy(snd.at[g, half], landed.at[half], out_sem.at[which])

    def compute(g, first, count):
        ext = exts[g]

        def row(r, carry):
            x = jnp.concatenate(
                [ext[idx_ref[r * K + k]] for k in range(K)], axis=1)
            y = jnp.dot(x, w[r].reshape(K * T, T), preferred_element_type=jnp.float32)
            at = pl.ds(pl.multiple_of(r * T, T), T)
            y = jnp.minimum(jnp.maximum(y + bias_ref[:, at], 0.0), 32.0)
            snd[g, r] = y.astype(snd.dtype)
            return carry

        lax.fori_loop(first, first + count, row, 0, unroll=UNROLL)

    for g in range(S):
        for which in (0, 1):
            for copy in hops(snd.at[g], g, 0, send_sem.at[g], which):
                copy.wait_recv()
        for which in (0, 1):
            first = which * (R // 2)
            if g == 0:
                for p in range(which * parts // 2, (which + 1) * parts // 2):
                    load(p).wait()
                    compute(g, p * rows_part, rows_part)
            else:
                compute(g, first, R // 2)

            @pl.when(s < S - 1)
            def _(g=g, which=which):
                for copy in hops(snd.at[g], g, s + 1, send_sem.at[g], which):
                    copy.start()

            @pl.when(s == S - 1)
            def _(g=g, which=which):
                if g == S - 1:
                    keep(g, which).start()
                else:
                    deliver(g, which).start()

    for which in (0, 1):
        mine, beside = hops(homes, 0, 0, home_sem, which)
        beside.wait_send()

        @pl.when(s > 0)
        def _(mine=mine):
            mine.wait_send()

        deliver(0, which).wait_recv()

    def unpacked(r, carry):
        out_ref[:, pl.ds(pl.multiple_of(r * T, T), T)] = landed[r]
        return carry

    lax.fori_loop(0, R, unpacked, 0, unroll=UNROLL)
    for g in range(S):
        for which in (0, 1):
            @pl.when(s < S - 1)
            def _(g=g, which=which):
                for copy in hops(snd.at[g], g, 0, send_sem.at[g], which):
                    copy.wait_send()

            if g < S - 1:
                @pl.when(s == S - 1)
                def _(g=g, which=which):
                    deliver(g, which).wait_send()


def shards(S, B, images, tile_weights, tile_columns, tile_counts, bias):
    rows, width = images.shape
    _, R, K, T, _ = tile_weights.shape
    first = lax.axis_index("blk") * R
    place = (tile_columns[0] - first + R // 2) % (R * B)
    live = jnp.arange(K, dtype=jnp.int32)[None, :] < tile_counts[0][:, None]
    idx = jnp.where(live, place, 2 * R).reshape(R * K)
    parts = 8
    vmem = pl.BlockSpec(memory_space=pltpu.VMEM)
    return pl.pallas_call(
        functools.partial(kernel, S, B, R, K, T, min(4, R // parts)),
        out_shape=jax.ShapeDtypeStruct((rows, width), images.dtype),
        in_specs=[pl.BlockSpec(memory_space=pltpu.SMEM), vmem, vmem, pl.BlockSpec(memory_space=pl.ANY)],
        out_specs=vmem,
        scratch_shapes=[
            pltpu.VMEM((R, K, T, T), tile_weights.dtype),
            pltpu.VMEM((R, rows, T), images.dtype),
            pltpu.VMEM((R, rows, T), images.dtype),
            pltpu.VMEM((S, R, rows, T), images.dtype),
            *[pltpu.VMEM((2 * R + 1, rows, T), images.dtype) for _ in range(S)],
            pltpu.SemaphoreType.DMA((parts,)),
            pltpu.SemaphoreType.DMA((4,)),
            pltpu.SemaphoreType.DMA((S, 4)),
            pltpu.SemaphoreType.DMA((S, 4)),
            pltpu.SemaphoreType.DMA((2,)),
        ],
        compiler_params=pltpu.CompilerParams(
            collective_id=0, has_side_effects=True, vmem_limit_bytes=52 * 2**20),
    )(idx, bias, images, tile_weights)


def solution(mesh):
    placed = (
        P("section", "blk"),
        P("section", "blk", None, None, None),
        P("section", "blk", None),
        P("section", "blk"),
        P("section", "blk"),
    )
    return jax.shard_map(
        functools.partial(shards, mesh.shape["section"], mesh.shape["blk"]),
        mesh=mesh, in_specs=placed, out_specs=P("section", "blk"), check_vma=False)
```

```python
import functools

import jax
import jax.numpy as jnp
from jax import lax
from jax.experimental import pallas as pl
from jax.experimental.pallas import tpu as pltpu
from jax.sharding import PartitionSpec as P

MESH = pl.DeviceIdType.MESH


def kernel(S, B, R, K, T, Q, UNROLL, idx_ref, bias_ref, images_ref, w_hbm, out_ref, w, homes, landed, snd, *rest):
    G = S * Q
    exts, (w_sem, home_sem, send_sem, recv_sem, out_sem) = rest[:G], rest[G:]
    s = lax.axis_index("section")
    b = lax.axis_index("blk")
    right, left = lax.rem(b + 1, B), lax.rem(b + B - 1, B)
    H = R // 2
    M = images_ref.shape[0] // Q
    parts = w_sem.shape[0]
    rows_part = R // parts

    def load(p):
        rows = pl.ds(p * rows_part, rows_part)
        return pltpu.make_async_copy(w_hbm.at[0, rows], w.at[rows], w_sem.at[p])

    for p in range(parts):
        load(p).start()

    barrier = pltpu.get_barrier_semaphore()

    def greet(d, carry):
        to = lax.rem(s + d, S)
        for place in (left, right):
            pl.semaphore_signal(barrier, inc=1, device_id=(to, place), device_id_type=MESH)

        @pl.when(d > 0)
        def _():
            pl.semaphore_signal(barrier, inc=1, device_id=(to, b), device_id_type=MESH)

        return carry

    lax.fori_loop(0, S, greet, 0)

    for ext in exts:
        ext[2 * R] = jnp.zeros(ext.shape[1:], ext.dtype)

    def packed(r, carry):
        block = images_ref[:, pl.ds(pl.multiple_of(r * T, T), T)]
        for q in range(Q):
            homes[q, r] = block[q * M:(q + 1) * M]
        return carry

    lax.fori_loop(0, R, packed, 0, unroll=4)
    pl.semaphore_wait(barrier, 3 * S - 1)

    def hops(src, g, to, sem, half):
        rows = src.at[pl.ds(half * H, H)]
        mine = pltpu.make_async_remote_copy(
            src_ref=rows, dst_ref=exts[g].at[pl.ds(H + half * H, H)], send_sem=sem.at[2 * half],
            recv_sem=recv_sem.at[g, 2 * half], device_id=(to, b), device_id_type=MESH)
        beside = pltpu.make_async_remote_copy(
            src_ref=rows, dst_ref=exts[g].at[pl.ds((1 - half) * 3 * H, H)], send_sem=sem.at[2 * half + 1],
            recv_sem=recv_sem.at[g, 2 * half + 1], device_id=(to, lax.rem(b + B - 1 + 2 * half, B)),
            device_id_type=MESH)
        return mine, beside

    def local(g, half):
        return pltpu.make_async_copy(
            homes.at[g, pl.ds(half * H, H)], exts[g].at[pl.ds(H + half * H, H)], recv_sem.at[g, 2 * half])

    for g in range(G):
        @pl.when(s == g // Q)
        def _(g=g):
            for half in (0, 1):
                mine, beside = hops(homes.at[g % Q], g, 0, home_sem.at[g % Q], half)
                if g < Q:
                    local(g, half).start()
                else:
                    mine.start()
                beside.start()

    def deliver(g, half):
        rows = pl.ds(half * H, H)
        return pltpu.make_async_remote_copy(
            src_ref=snd.at[g, rows], dst_ref=landed.at[g % Q, rows], send_sem=send_sem.at[g, 2 * half],
            recv_sem=out_sem.at[g % Q, half], device_id=(g // Q, b), device_id_type=MESH)

    def keep(g, half):
        rows = pl.ds(half * H, H)
        return pltpu.make_async_copy(snd.at[g, rows], landed.at[g % Q, rows], out_sem.at[g % Q, half])

    def stage(g):
        ext = exts[g]

        def row(r, carry):
            x = jnp.concatenate([ext[idx_ref[r * K + k]] for k in range(K)], axis=1)
            y = jnp.dot(x, w[r].reshape(K * T, T), preferred_element_type=jnp.float32)
            y = y + bias_ref[:, pl.ds(pl.multiple_of(r * T, T), T)]
            snd[g, r] = jnp.minimum(jnp.maximum(y, 0.0), 32.0).astype(snd.dtype)
            return carry

        def halves(half, carry):
            if g == 0:
                for p in range(parts // 2):
                    load(half * (parts // 2) + p).wait()
            lax.fori_loop(half * (H // UNROLL), (half + 1) * (H // UNROLL), rows, 0)

            @pl.when(s < S - 1)
            def _():
                for copy in hops(snd.at[g], g, s + 1, send_sem.at[g], half):
                    copy.start()

            @pl.when(s == S - 1)
            def _():
                (keep if g // Q == S - 1 else deliver)(g, half).start()

            return carry

        def rows(i, carry):
            for j in range(UNROLL):
                row(i * UNROLL + j, 0)
            return carry

        lax.fori_loop(0, 2, halves, 0)

    for g in range(G):
        for half in (0, 1):
            for copy in hops(snd.at[g], g, 0, send_sem.at[g], half):
                copy.wait_recv()
        stage(g)

    for q in range(Q):
        for half in (0, 1):
            mine, beside = hops(homes.at[q], q, 0, home_sem.at[q], half)
            beside.wait_send()

            @pl.when(s > 0)
            def _(mine=mine):
                mine.wait_send()

            deliver(q, half).wait_recv()

    def unpacked(r, carry):
        out_ref[:, pl.ds(pl.multiple_of(r * T, T), T)] = jnp.concatenate([landed[q, r] for q in range(Q)], axis=0)
        return carry

    lax.fori_loop(0, R, unpacked, 0, unroll=4)
    for g in range(G):
        for half in (0, 1):
            @pl.when(s < S - 1)
            def _(g=g, half=half):
                for copy in hops(snd.at[g], g, 0, send_sem.at[g], half):
                    copy.wait_send()

            if g // Q < S - 1:
                @pl.when(s == S - 1)
                def _(g=g, half=half):
                    deliver(g, half).wait_send()


def shards(S, B, images, tile_weights, tile_columns, tile_counts, bias):
    rows, width = images.shape
    _, R, K, T, _ = tile_weights.shape
    first = lax.axis_index("blk") * R
    place = (tile_columns[0] - first + R // 2) % (R * B)
    live = jnp.arange(K, dtype=jnp.int32)[None, :] < tile_counts[0][:, None]
    idx = jnp.where(live, place, 2 * R).reshape(R * K)
    parts = 8
    Q = 2 if rows % 8 == 0 else 1
    M, G = rows // Q, S * Q
    vmem = pl.BlockSpec(memory_space=pltpu.VMEM)
    return pl.pallas_call(
        functools.partial(kernel, S, B, R, K, T, Q, max(1, min(R // 2, 256 // S))),
        out_shape=jax.ShapeDtypeStruct((rows, width), images.dtype),
        in_specs=[pl.BlockSpec(memory_space=pltpu.SMEM), vmem, vmem, pl.BlockSpec(memory_space=pl.ANY)],
        out_specs=vmem,
        scratch_shapes=[
            pltpu.VMEM((R, K, T, T), tile_weights.dtype),
            pltpu.VMEM((Q, R, M, T), images.dtype),
            pltpu.VMEM((Q, R, M, T), images.dtype),
            pltpu.VMEM((G, R, M, T), images.dtype),
            *[pltpu.VMEM((2 * R + 1, M, T), images.dtype) for _ in range(G)],
            pltpu.SemaphoreType.DMA((parts,)),
            pltpu.SemaphoreType.DMA((Q, 4)),
            pltpu.SemaphoreType.DMA((G, 4)),
            pltpu.SemaphoreType.DMA((G, 4)),
            pltpu.SemaphoreType.DMA((Q, 2)),
        ],
        compiler_params=pltpu.CompilerParams(
            collective_id=0, has_side_effects=True, vmem_limit_bytes=52 * 2**20),
    )(idx, bias, images, tile_weights)


def solution(mesh):
    placed = (
        P("section", "blk"),
        P("section", "blk", None, None, None),
        P("section", "blk", None),
        P("section", "blk"),
        P("section", "blk"),
    )
    return jax.shard_map(
        functools.partial(shards, mesh.shape["section"], mesh.shape["blk"]),
        mesh=mesh, in_specs=placed, out_specs=P("section", "blk"), check_vma=False)
```

```python
import functools

import jax
import jax.numpy as jnp
from jax import lax
from jax.experimental import pallas as pl
from jax.experimental.pallas import tpu as pltpu
from jax.sharding import PartitionSpec as P

MESH = pl.DeviceIdType.MESH


def kernel(S, B, R, K, T, Q, UNROLL, idx_ref, bias_ref, images_ref, w_hbm, out_ref, w, homes, landed, snd, *rest):
    G = S * Q
    exts, (w_sem, home_sem, send_sem, recv_sem, out_sem) = rest[:G], rest[G:]
    s = lax.axis_index("section")
    b = lax.axis_index("blk")
    right, left = lax.rem(b + 1, B), lax.rem(b + B - 1, B)
    H, C = R // 2, 4
    L = R // C
    M = images_ref.shape[0] // Q
    parts = w_sem.shape[0]
    rows_part = R // parts

    def load(p):
        rows = pl.ds(p * rows_part, rows_part)
        return pltpu.make_async_copy(w_hbm.at[0, rows], w.at[rows], w_sem.at[p])

    for p in range(parts):
        load(p).start()

    barrier = pltpu.get_barrier_semaphore()

    def greet(d, carry):
        to = lax.rem(s + d, S)
        for place in (left, right):
            pl.semaphore_signal(barrier, inc=1, device_id=(to, place), device_id_type=MESH)

        @pl.when(d > 0)
        def _():
            pl.semaphore_signal(barrier, inc=1, device_id=(to, b), device_id_type=MESH)

        return carry

    lax.fori_loop(0, S, greet, 0)

    for ext in exts:
        ext[2 * R] = jnp.zeros(ext.shape[1:], ext.dtype)

    def packed(r, carry):
        block = images_ref[:, pl.ds(pl.multiple_of(r * T, T), T)]
        for q in range(Q):
            homes[q, r] = block[q * M:(q + 1) * M]
        return carry

    lax.fori_loop(0, R, packed, 0, unroll=4)
    pl.semaphore_wait(barrier, 3 * S - 1)

    def hops(src, g, to, sem, part):
        rows = src.at[pl.ds(part * L, L)]
        mine = pltpu.make_async_remote_copy(
            src_ref=rows, dst_ref=exts[g].at[pl.ds(H + part * L, L)], send_sem=sem.at[2 * part],
            recv_sem=recv_sem.at[g, 2 * part], device_id=(to, b), device_id_type=MESH)
        beside = pltpu.make_async_remote_copy(
            src_ref=rows, dst_ref=exts[g].at[pl.ds((part * L + 3 * H) % (4 * H), L)], send_sem=sem.at[2 * part + 1],
            recv_sem=recv_sem.at[g, 2 * part + 1], device_id=(to, lax.rem(b + B - 1 + 2 * (part // (C // 2)), B)),
            device_id_type=MESH)
        return beside, mine

    def local(g, part):
        return pltpu.make_async_copy(
            homes.at[g, pl.ds(part * L, L)], exts[g].at[pl.ds(H + part * L, L)], recv_sem.at[g, 2 * part])

    for g in range(G):
        @pl.when(s == g // Q)
        def _(g=g):
            for part in range(C):
                beside, mine = hops(homes.at[g % Q], g, 0, home_sem.at[g % Q], part)
                beside.start()
                if g < Q:
                    local(g, part).start()
                else:
                    mine.start()

    def deliver(g, part):
        rows = pl.ds(part * L, L)
        return pltpu.make_async_remote_copy(
            src_ref=snd.at[g, rows], dst_ref=landed.at[g % Q, rows], send_sem=send_sem.at[g, 2 * part],
            recv_sem=out_sem.at[g % Q, part], device_id=(g // Q, b), device_id_type=MESH)

    def keep(g, part):
        rows = pl.ds(part * L, L)
        return pltpu.make_async_copy(snd.at[g, rows], landed.at[g % Q, rows], out_sem.at[g % Q, part])

    def stage(g):
        ext = exts[g]

        def row(r, carry):
            x = jnp.concatenate([ext[idx_ref[r * K + k]] for k in range(K)], axis=1)
            y = jnp.dot(x, w[r].reshape(K * T, T), preferred_element_type=jnp.float32)
            y = y + bias_ref[:, pl.ds(pl.multiple_of(r * T, T), T)]
            snd[g, r] = jnp.minimum(jnp.maximum(y, 0.0), 32.0).astype(snd.dtype)
            return carry

        def quarters(part, carry):
            if g == 0:
                for p in range(parts // C):
                    load(part * (parts // C) + p).wait()
            lax.fori_loop(part * (L // UNROLL), (part + 1) * (L // UNROLL), rows, 0)

            @pl.when(s < S - 1)
            def _():
                for copy in hops(snd.at[g], g, s + 1, send_sem.at[g], part):
                    copy.start()

            @pl.when(s == S - 1)
            def _():
                (keep if g // Q == S - 1 else deliver)(g, part).start()

            return carry

        def rows(i, carry):
            for j in range(UNROLL):
                row(i * UNROLL + j, 0)
            return carry

        lax.fori_loop(0, C, quarters, 0)

    for g in range(G):
        for part in range(C):
            for copy in hops(snd.at[g], g, 0, send_sem.at[g], part):
                copy.wait_recv()
        stage(g)

    for q in range(Q):
        for part in range(C):
            beside, mine = hops(homes.at[q], q, 0, home_sem.at[q], part)
            beside.wait_send()

            @pl.when(s > 0)
            def _(mine=mine):
                mine.wait_send()

            deliver(q, part).wait_recv()

    def unpacked(r, carry):
        out_ref[:, pl.ds(pl.multiple_of(r * T, T), T)] = jnp.concatenate([landed[q, r] for q in range(Q)], axis=0)
        return carry

    lax.fori_loop(0, R, unpacked, 0, unroll=4)
    for g in range(G):
        for part in range(C):
            @pl.when(s < S - 1)
            def _(g=g, part=part):
                for copy in hops(snd.at[g], g, 0, send_sem.at[g], part):
                    copy.wait_send()

            if g // Q < S - 1:
                @pl.when(s == S - 1)
                def _(g=g, part=part):
                    deliver(g, part).wait_send()


def shards(S, B, images, tile_weights, tile_columns, tile_counts, bias):
    rows, width = images.shape
    _, R, K, T, _ = tile_weights.shape
    first = lax.axis_index("blk") * R
    place = (tile_columns[0] - first + R // 2) % (R * B)
    live = jnp.arange(K, dtype=jnp.int32)[None, :] < tile_counts[0][:, None]
    idx = jnp.where(live, place, 2 * R).reshape(R * K)
    parts = 8
    Q = 2 if rows % 8 == 0 else 1
    M, G = rows // Q, S * Q
    vmem = pl.BlockSpec(memory_space=pltpu.VMEM)
    return pl.pallas_call(
        functools.partial(kernel, S, B, R, K, T, Q, max(1, min(R // 4, 256 // S))),
        out_shape=jax.ShapeDtypeStruct((rows, width), images.dtype),
        in_specs=[pl.BlockSpec(memory_space=pltpu.SMEM), vmem, vmem, pl.BlockSpec(memory_space=pl.ANY)],
        out_specs=vmem,
        scratch_shapes=[
            pltpu.VMEM((R, K, T, T), tile_weights.dtype),
            pltpu.VMEM((Q, R, M, T), images.dtype),
            pltpu.VMEM((Q, R, M, T), images.dtype),
            pltpu.VMEM((G, R, M, T), images.dtype),
            *[pltpu.VMEM((2 * R + 1, M, T), images.dtype) for _ in range(G)],
            pltpu.SemaphoreType.DMA((parts,)),
            pltpu.SemaphoreType.DMA((Q, 8)),
            pltpu.SemaphoreType.DMA((G, 8)),
            pltpu.SemaphoreType.DMA((G, 8)),
            pltpu.SemaphoreType.DMA((Q, 4)),
        ],
        compiler_params=pltpu.CompilerParams(
            collective_id=0, has_side_effects=True, vmem_limit_bytes=52 * 2**20),
    )(idx, bias, images, tile_weights)


def solution(mesh):
    placed = (
        P("section", "blk"),
        P("section", "blk", None, None, None),
        P("section", "blk", None),
        P("section", "blk"),
        P("section", "blk"),
    )
    return jax.shard_map(
        functools.partial(shards, mesh.shape["section"], mesh.shape["blk"]),
        mesh=mesh, in_specs=placed, out_specs=P("section", "blk"), check_vma=False)
```
